32 devices in a mesh: gx: 16 (over z, y, core), gy: 2 (over x).
Axes of the slice: x: 2, y: 2, z: 4, core: 2. Of those that a mesh axis runs over, the one named last changes fastest.
Arguments:
- tokens: bfloat16 [512, 6144], P('gx', 'gy'), may hold values from -30 to 30
- ln_gain: float32 [6144], P('gy'), may hold values from 0.1 to 1.9
- oft_skew: float32 [8, 24, 256, 256], P(None, 'gy'), may hold values from -0.375 to 0.375
- tenant_of_image: int32 [2], replicated, may hold values from 0 to 7
- w_qkv: bfloat16 [6144, 32, 3, 128], P('gy', 'gx'), may hold values from -0.076546554 to 0.076546554
- w_up: bfloat16 [6144, 24576], P('gy', 'gx'), may hold values from -0.078125 to 0.078125
- up_bias: float32 [24576], P('gx'), may hold values from -3 to 3
- q_gain: float32 [32, 128], P('gx'), may hold values from 0.8 to 5
- k_gain: float32 [32, 128], P('gx'), may hold values from 0.8 to 5
- w_out: bfloat16 [32, 128, 6144], P('gx', None, 'gy'), may hold values from -0.09375 to 0.09375
- w_down: bfloat16 [24576, 6144], P('gx', 'gy'), may hold values from -0.0390625 to 0.0390625
- down_bias: float32 [6144], P('gy'), may hold values from -3 to 3
Outputs:
- layer_out: bfloat16 [512, 6144], P('gx', 'gy')
The draws below stay inside these ranges and needn't reach their ends.
All inputs are finite; a program needn't handle non-finite values.
Results may differ from the reference program's by a relative error of at most 0.005.
Values may be sent and summed in bfloat16 or wider, within the bound.
A program may use at most 128 MiB of HBM per device.

```python
import jax
import jax.numpy as jnp
from jax import lax

D = 6144
FF = 24576
DH = 128
HEADS = 32
OFT_BLOCK = 256
TENANTS = 8
PATCHES = 256
IMAGES = 2
TOKENS = 512


def draw_tokens(key, part):
    first, second = jax.random.split(key, 2)
    column_scale = 0.5 * 3.0 ** (jnp.arange(D, dtype=jnp.float32) / D)
    column_scale = column_scale[None, :] * jax.random.uniform(second, (1, D), jnp.float32, 0.7, 1.3)
    drawn = jax.random.normal(first, (TOKENS, D), jnp.float32) * column_scale
    return jnp.clip(drawn, -30.0, 30.0).astype(jnp.bfloat16)


def draw_oft_skew(key, part):
    first = jax.random.fold_in(jax.random.fold_in(key, 37), 0)
    block_count = D // OFT_BLOCK
    shape = (TENANTS, block_count, OFT_BLOCK, OFT_BLOCK)
    drawn = jax.random.uniform(first, shape, jnp.float32, -0.375, 0.375)
    return drawn.astype(jnp.float32)


def draw_w_qkv(key, part):
    first = jax.random.fold_in(key, 0)
    base = jnp.clip(jax.random.normal(first, (D, HEADS, 3, DH), jnp.float32), -5.5, 5.5)
    return (base * D ** (-0.5)).astype(jnp.bfloat16)


def gain_draw(key, salt):
    folded = jax.random.fold_in(key, salt)
    second = jax.random.fold_in(folded, 1)
    return jax.random.uniform(second, (HEADS, DH), jnp.float32, 0.8, 1.6)


def draw_q_gain(key, part):
    return gain_draw(key, 11)


def draw_k_gain(key, part):
    return gain_draw(key, 23)


def block_scale(key, extent, cuts, smallest, largest):
    level, own = 1.0, jax.random.fold_in(key, 6)
    for axis_at, parts in cuts:
        heights = jnp.exp(jax.random.uniform(jax.random.fold_in(own, axis_at), (parts,), jnp.float32, smallest / len(cuts), largest / len(cuts)))
        level = level * jnp.repeat(heights, extent[axis_at] // parts).reshape([-1 if axis == axis_at else 1 for axis in range(len(extent))])
    return level


def normal_values(stream_key, extent, spread, limit, cuts=(), kind=jnp.bfloat16):
    result = jax.random.normal(stream_key, extent, jnp.float32) * spread
    if len(cuts) > 0:
        result = block_scale(stream_key, extent, cuts, -0.22, 0.18) * result
    return jnp.clip(result, min=-limit, max=limit).astype(kind)


def setup_inputs(seed: int = 0) -> dict:
    key_of = jax.random.split(jax.random.key(seed), 13)
    return {
        "tokens": draw_tokens(jax.random.fold_in(key_of[12], 71), 0),
        "ln_gain": jnp.clip(1.0 + 0.18 * jax.random.normal(key_of[1], (D,), jnp.float32), 0.1, 1.9),
        "oft_skew": draw_oft_skew(jax.random.fold_in(key_of[12], 71), 0),
        "tenant_of_image": jax.random.randint(key_of[3], (IMAGES,), 0, TENANTS).astype(jnp.int32),
        "w_qkv": draw_w_qkv(jax.random.fold_in(key_of[12], 71), 0),
        "w_up": normal_values(key_of[5], (D, FF), D ** -0.5, 0.078125, ((0, 2), (1, 16))),
        "up_bias": normal_values(key_of[6], (FF,), 0.5, 3.0, ((0, 16),), jnp.float32),
        "q_gain": draw_q_gain(jax.random.fold_in(key_of[12], 71), 0),
        "k_gain": draw_k_gain(jax.random.fold_in(key_of[12], 71), 0),
        "w_out": normal_values(key_of[9], (HEADS, DH, D), (HEADS * DH) ** -0.5, 0.09375, ((0, 16), (2, 2))),
        "w_down": normal_values(key_of[10], (FF, D), FF ** -0.5, 0.0390625, ((0, 16), (1, 2))),
        "down_bias": normal_values(key_of[11], (D,), 0.5, 3.0, ((0, 2),), jnp.float32),
    }


HIGH = lax.Precision.HIGHEST

def cayley(skew_raw):
    skew_part = 0.5 * (skew_raw - jnp.swapaxes(skew_raw, -1, -2))
    identity = jnp.eye(skew_part.shape[-1], dtype=jnp.float32)
    plus_skew = identity + skew_part
    gram_matrix = identity - jnp.matmul(skew_part, skew_part, precision=HIGH)
    factor = jnp.linalg.cholesky(gram_matrix)
    lower_solved = lax.linalg.triangular_solve(factor, plus_skew, left_side=True, lower=True)
    solved = lax.linalg.triangular_solve(factor, lower_solved, left_side=True, lower=True, transpose_a=True)
    return jnp.matmul(plus_skew, solved, precision=HIGH)

def norm_last(values_in, gain):
    width_count = values_in.shape[-1]
    row_mean = lax.optimization_barrier(jnp.sum(values_in, -1, keepdims=True)) / width_count
    row_var = lax.optimization_barrier(jnp.sum(values_in * values_in, -1, keepdims=True)) / width_count - row_mean * row_mean
    return (values_in - row_mean) * lax.rsqrt(row_var + 1e-06) * gain

def reference(tokens, ln_gain, oft_skew, tenant_of_image, w_qkv, w_up, up_bias, q_gain, k_gain, w_out, w_down, down_bias):
    floats = tokens.astype(jnp.float32)
    normed = norm_last(floats, ln_gain)
    block_count = D // OFT_BLOCK
    rotations = cayley(oft_skew.reshape(TENANTS * block_count, OFT_BLOCK, OFT_BLOCK))
    rotations = rotations.reshape(TENANTS, block_count, OFT_BLOCK, OFT_BLOCK)
    chosen = rotations[tenant_of_image.astype(jnp.int32)]
    blocks = normed.reshape(IMAGES, PATCHES, block_count, OFT_BLOCK)
    turned = jnp.einsum('ipnb,incb->ipnc', blocks, chosen, precision=HIGH)
    turned = turned.reshape(TOKENS, D).astype(jnp.bfloat16)
    projected = jnp.dot(turned.astype(jnp.float32), w_qkv.reshape(D, HEADS * 3 * DH).astype(jnp.float32), preferred_element_type=jnp.float32)
    projected = projected.reshape(IMAGES, PATCHES, HEADS, 3, DH)
    up_pre = jnp.dot(turned.astype(jnp.float32), w_up.astype(jnp.float32), preferred_element_type=jnp.float32)
    queries = norm_last(projected[:, :, :, 0, :], q_gain).astype(jnp.bfloat16)
    keys_normed = norm_last(projected[:, :, :, 1, :], k_gain).astype(jnp.bfloat16)
    values = projected[:, :, :, 2, :].astype(jnp.bfloat16)
    scores = jnp.einsum('iphd,iqhd->ihpq', queries.astype(jnp.float32), keys_normed.astype(jnp.float32)) / jnp.sqrt(jnp.float32(DH))
    top_score = lax.optimization_barrier(jnp.max(scores, -1, keepdims=True))
    expo = jnp.exp(scores - top_score)
    weights = (expo / lax.optimization_barrier(jnp.sum(expo, -1, keepdims=True))).astype(jnp.bfloat16)
    attended = jnp.einsum('ihpq,iqhd->iphd', weights.astype(jnp.float32), values.astype(jnp.float32))
    attended = attended.astype(jnp.bfloat16).reshape(TOKENS, HEADS * DH)
    hidden = jax.nn.gelu(up_pre + up_bias, approximate=False).astype(jnp.bfloat16)
    mixed = jnp.dot(attended.astype(jnp.float32), w_out.reshape(HEADS * DH, D).astype(jnp.float32), preferred_element_type=jnp.float32)
    mixed = mixed + jnp.dot(hidden.astype(jnp.float32), w_down.astype(jnp.float32), preferred_element_type=jnp.float32)
    return (floats + mixed + down_bias).astype(jnp.bfloat16)
```

```python
import functools

import jax
import jax.numpy as jnp
from jax import lax
from jax.experimental import pallas as pl
from jax.experimental.pallas import tpu as pltpu
from jax.sharding import PartitionSpec as P

PATCHES = 256
HIGH = lax.Precision.HIGHEST
F32 = jnp.float32
BF16 = jnp.bfloat16


def split(a):
    high = a.astype(BF16)
    return high, (a - high.astype(F32)).astype(BF16)


def dot3(a, b):
    dot = functools.partial(jnp.dot, preferred_element_type=F32)
    return dot(a[0], b[0]) + (dot(a[0], b[1]) + dot(a[1], b[0]))


def inverse_kernel(per, tenant_ref, skew_ref, out_ref, gen_hi, gen_lo, x_ref):
    size = skew_ref.shape[-1]
    rows = lax.broadcasted_iota(jnp.int32, (size, size), 0)
    cols = lax.broadcasted_iota(jnp.int32, (size, size), 1)
    eye = (rows == cols).astype(F32)
    bound = jnp.float32(0.0)
    for k in range(per):
        raw = skew_ref[0, k]
        skew = 0.5 * (raw - raw.T)
        pair = split(skew)
        square = dot3(pair, pair)
        bound = jnp.maximum(bound, jnp.sum(square * square))
        whole = split(eye + skew)
        gen_hi[k] = whole[0]
        gen_lo[k] = whole[1]
        x_ref[k] = eye - skew
    top = 1.001 * jnp.sqrt(jnp.full((8, 128), 0.5 * bound, F32)) + 1e-3
    low = 2.0 / (2.0 + top)
    for k in range(per):
        x_ref[k] = x_ref[k] * low[0:1, 0:1]

    def more(state):
        return state[1] < 1.0 - 1e-6

    def step(state):
        low, _ = state
        grown = low * (2.0 - low)
        scale = 2.0 / (1.0 + grown)
        xs = [split(x_ref[k]) for k in range(per)]
        ys = [dot3((gen_hi[k], gen_lo[k]), xs[k]) for k in range(per)]
        rest = [split(2.0 * eye - y) for y in ys]
        for k in range(per):
            x_ref[k] = dot3(xs[k], rest[k]) * scale[0:1, 0:1]
        low = jnp.minimum(scale * grown, 1.0)
        return low, jnp.max(low)

    lax.while_loop(more, step, (low, jnp.max(low)))
    for k in range(per):
        out_ref[k] = 2.0 * x_ref[k] - eye


def turning(oft_skew, tenant):
    _, count, size, _ = oft_skew.shape
    per = next(p for p in (4, 3, 2, 1) if count % p == 0)
    return pl.pallas_call(
        functools.partial(inverse_kernel, per),
        out_shape=jax.ShapeDtypeStruct((count, size, size), F32),
        grid_spec=pltpu.PrefetchScalarGridSpec(
            num_scalar_prefetch=1,
            grid=(count // per,),
            in_specs=[pl.BlockSpec((1, per, size, size), lambda i, t: (t[0], i, 0, 0))],
            out_specs=pl.BlockSpec((per, size, size), lambda i, t: (i, 0, 0)),
            scratch_shapes=[
                pltpu.VMEM((per, size, size), BF16),
                pltpu.VMEM((per, size, size), BF16),
                pltpu.VMEM((per, size, size), F32),
            ],
        ),
        compiler_params=pltpu.CompilerParams(vmem_limit_bytes=32 * 2**20),
        cost_estimate=pl.CostEstimate(flops=count * 50 * 2 * size**3, bytes_accessed=count * 8 * size**2, transcendentals=0),
    )(tenant.reshape(1), oft_skew)


def lay_kernel(ways, w_ref, out_ref):
    block = 64
    size = ways * block
    rows = lax.broadcasted_iota(jnp.int32, (size, size), 0)
    cols = lax.broadcasted_iota(jnp.int32, (size, size), 1)
    move = (cols == (rows % block) * ways + rows // block).astype(BF16)
    for k in range(out_ref.shape[0] // block):
        laid = jnp.dot(move, w_ref[k * size : (k + 1) * size, :], preferred_element_type=F32).astype(BF16)
        for c in range(ways):
            out_ref[k * block : (k + 1) * block, c * 128 : (c + 1) * 128] = laid[c * block : (c + 1) * block, :]


def lay_qkv(w_qkv):
    depth, heads, three, dim = w_qkv.shape
    ways = heads * three
    turned = w_qkv.transpose(0, 2, 1, 3)
    if heads != 2 or dim != 128 or depth % 512:
        return turned.reshape(depth, ways * dim)
    return pl.pallas_call(
        functools.partial(lay_kernel, ways),
        out_shape=jax.ShapeDtypeStruct((depth, ways * dim), BF16),
        grid=(depth // 512,),
        in_specs=[pl.BlockSpec((512 * ways, dim), lambda i: (i, 0))],
        out_specs=pl.BlockSpec((512, ways * dim), lambda i: (i, 0)),
        cost_estimate=pl.CostEstimate(flops=2 * depth * ways * dim * 384, bytes_accessed=4 * depth * ways * dim, transcendentals=0),
    )(turned.reshape(depth * ways, dim))


def head_norm(values_in, gain):
    width_count = values_in.shape[-1]
    row_mean = jnp.sum(values_in, -1, keepdims=True) / width_count
    row_var = jnp.sum(values_in * values_in, -1, keepdims=True) / width_count - row_mean * row_mean
    return (values_in - row_mean) * lax.rsqrt(row_var + 1e-06) * gain


def attention(qkv, q_gain, k_gain):
    heads, dim = q_gain.shape
    count = qkv.shape[0] // PATCHES
    parts = qkv.reshape(count, PATCHES, 3, heads, dim)
    queries = head_norm(parts[:, :, 0], q_gain).astype(BF16)
    keys_normed = head_norm(parts[:, :, 1], k_gain).astype(BF16)
    values = parts[:, :, 2].astype(BF16)
    scores = jnp.einsum("iphd,iqhd->ihpq", queries, keys_normed, preferred_element_type=F32) / jnp.sqrt(F32(dim))
    expo = jnp.exp(scores - jnp.max(scores, -1, keepdims=True))
    weights = (expo / jnp.sum(expo, -1, keepdims=True)).astype(BF16)
    attended = jnp.einsum("ihpq,iqhd->iphd", weights, values, preferred_element_type=F32)
    return attended.astype(BF16).reshape(-1, heads * dim)


def per_device(
    tokens, ln_gain, oft_skew, tenant_of_image, w_qkv, w_up, up_bias, q_gain, k_gain, w_out, w_down, down_bias
):
    row_count, local_width = tokens.shape
    ways = lax.axis_size("gy")
    full_width = local_width * ways
    gx, gy = lax.axis_index("gx"), lax.axis_index("gy")
    dot = functools.partial(jnp.dot, preferred_element_type=F32)

    tenant = lax.dynamic_index_in_dim(tenant_of_image, gx * row_count // PATCHES, 0, keepdims=False)
    rotation = turning(oft_skew, tenant)
    floats = tokens.astype(F32)
    sums = jnp.stack([jnp.sum(floats, 1), jnp.sum(floats * floats, 1)])
    if ways == 2:
        swap = functools.partial(lax.ppermute, axis_name="gy", perm=[(0, 1), (1, 0)])
        sums = sums + swap(sums)
    else:
        sums = lax.psum(sums, "gy")
    row_mean = sums[0][:, None] / full_width
    row_var = sums[1][:, None] / full_width - row_mean * row_mean
    normed = (floats - row_mean) * lax.rsqrt(row_var + 1e-06) * ln_gain
    count, size = rotation.shape[:2]
    turned = jnp.einsum("pnb,nbc->pnc", normed.reshape(row_count, count, size), rotation, precision=HIGH)
    turned = turned.reshape(row_count, local_width).astype(BF16)
    w_first = lay_qkv(w_qkv)
    every = lax.all_gather(turned, "gx", axis=0, tiled=True)

    qkv_cols, up_cols = w_first.shape[1], w_up.shape[1]
    w_attn = w_out.reshape(-1, w_out.shape[2])
    if ways == 2:
        half = every.shape[0] // 2
        mine = lax.dynamic_slice_in_dim(every, gy * half, half, 0)
        theirs = lax.dynamic_slice_in_dim(every, (1 - gy) * half, half, 0)
        cut = up_cols // 3
        pieces = [w_first] + [w_up[:, k * cut : (k + 1) * cut] for k in range(3)]
        got = [swap(dot(theirs, w).astype(BF16)) for w in pieces]
        own = [dot(mine, w) for w in pieces]
        summed = [a + b.astype(F32) for a, b in zip(own, got)]
        acts = [attention(summed[0], q_gain, k_gain)]
        for k in range(3):
            pre = summed[k + 1] + up_bias[k * cut : (k + 1) * cut]
            acts.append(jax.nn.gelu(pre, approximate=False).astype(BF16))
        others = [swap(a) for a in acts]
        mixed_own = dot(acts[0], w_attn) + dot(jnp.concatenate(acts[1:], 1), w_down)
        mixed_other = dot(others[0], w_attn) + dot(jnp.concatenate(others[1:], 1), w_down)
        mixed_own, mixed_other = mixed_own.astype(BF16), mixed_other.astype(BF16)
        first = gy == 0
        mixed = jnp.concatenate(
            [jnp.where(first, mixed_own, mixed_other), jnp.where(first, mixed_other, mixed_own)], 0
        )
    else:
        part = jnp.concatenate([dot(every, w_first), dot(every, w_up)], 1)
        summed = lax.psum_scatter(part.astype(BF16), "gy", scatter_dimension=0, tiled=True).astype(F32)
        acts = jnp.concatenate(
            [
                attention(summed[:, :qkv_cols], q_gain, k_gain),
                jax.nn.gelu(summed[:, qkv_cols:] + up_bias, approximate=False).astype(BF16),
            ],
            1,
        )
        acts = lax.all_gather(acts, "gy", axis=0, tiled=True)
        heads_cols = w_attn.shape[0]
        mixed = (dot(acts[:, :heads_cols], w_attn) + dot(acts[:, heads_cols:], w_down)).astype(BF16)
    mixed = lax.psum_scatter(mixed, "gx", scatter_dimension=0, tiled=True)
    return (floats + mixed.astype(F32) + down_bias).astype(BF16)


def solution(mesh):
    in_specs = (
        P("gx", "gy"),
        P("gy"),
        P(None, "gy", None, None),
        P(),
        P("gy", "gx", None, None),
        P("gy", "gx"),
        P("gx"),
        P("gx", None),
        P("gx", None),
        P("gx", None, "gy"),
        P("gx", "gy"),
        P("gy"),
    )
    return jax.shard_map(per_device, mesh=mesh, in_specs=in_specs, out_specs=P("gx", "gy"), check_vma=False)
```

```python
import functools

import jax
import jax.numpy as jnp
from jax import lax
from jax.experimental import pallas as pl
from jax.experimental.pallas import tpu as pltpu
from jax.sharding import PartitionSpec as P

PATCHES = 256
HIGH = lax.Precision.HIGHEST
F32 = jnp.float32
BF16 = jnp.bfloat16


def split(a):
    high = a.astype(BF16)
    return high, (a - high.astype(F32)).astype(BF16)


def dot3(a, b):
    dot = functools.partial(jnp.dot, preferred_element_type=F32)
    return dot(a[0], b[0]) + (dot(a[0], b[1]) + dot(a[1], b[0]))


def inverse_kernel(per, tenant_ref, skew_ref, out_ref, gen_hi, gen_lo, x_ref):
    size = skew_ref.shape[-1]
    rows = lax.broadcasted_iota(jnp.int32, (size, size), 0)
    cols = lax.broadcasted_iota(jnp.int32, (size, size), 1)
    eye = (rows == cols).astype(F32)
    bound = jnp.float32(0.0)
    for k in range(per):
        raw = skew_ref[0, k]
        skew = 0.5 * (raw - raw.T)
        pair = split(skew)
        square = dot3(pair, pair)
        bound = jnp.maximum(bound, jnp.sum(square * square))
        whole = split(eye + skew)
        gen_hi[k] = whole[0]
        gen_lo[k] = whole[1]
        x_ref[k] = eye - skew
    top = 1.001 * jnp.sqrt(jnp.full((8, 128), 0.5 * bound, F32)) + 1e-3
    low = 2.0 / (2.0 + top)
    for k in range(per):
        x_ref[k] = x_ref[k] * low[0:1, 0:1]

    def more(state):
        return state[1] < 1.0 - 1e-6

    def step(state):
        low, _ = state
        grown = low * (2.0 - low)
        scale = 2.0 / (1.0 + grown)
        xs = [split(x_ref[k]) for k in range(per)]
        ys = [dot3((gen_hi[k], gen_lo[k]), xs[k]) for k in range(per)]
        rest = [split(2.0 * eye - y) for y in ys]
        for k in range(per):
            x_ref[k] = dot3(xs[k], rest[k]) * scale[0:1, 0:1]
        low = jnp.minimum(scale * grown, 1.0)
        return low, jnp.max(low)

    lax.while_loop(more, step, (low, jnp.max(low)))
    for k in range(per):
        out_ref[k] = 2.0 * x_ref[k] - eye


def turning(oft_skew, tenant, shares=1, share=0):
    _, count, size, _ = oft_skew.shape
    count = count // shares
    per = next(p for p in (4, 3, 2, 1) if count % p == 0)
    return pl.pallas_call(
        functools.partial(inverse_kernel, per),
        out_shape=jax.ShapeDtypeStruct((count, size, size), F32),
        grid_spec=pltpu.PrefetchScalarGridSpec(
            num_scalar_prefetch=1,
            grid=(count // per,),
            in_specs=[pl.BlockSpec((1, per, size, size), lambda i, t: (t[0], t[1] + i, 0, 0))],
            out_specs=pl.BlockSpec((per, size, size), lambda i, t: (i, 0, 0)),
            scratch_shapes=[
                pltpu.VMEM((per, size, size), BF16),
                pltpu.VMEM((per, size, size), BF16),
                pltpu.VMEM((per, size, size), F32),
            ],
        ),
        compiler_params=pltpu.CompilerParams(vmem_limit_bytes=32 * 2**20),
        cost_estimate=pl.CostEstimate(flops=count * 50 * 2 * size**3, bytes_accessed=count * 8 * size**2, transcendentals=0),
    )(jnp.stack([tenant, jnp.int32(share * (count // per))]), oft_skew)


def lay_kernel(ways, w_ref, out_ref):
    block = 64
    size = ways * block
    rows = lax.broadcasted_iota(jnp.int32, (size, size), 0)
    cols = lax.broadcasted_iota(jnp.int32, (size, size), 1)
    move = (cols == (rows % block) * ways + rows // block).astype(BF16)
    for k in range(out_ref.shape[0] // block):
        laid = jnp.dot(move, w_ref[k * size : (k + 1) * size, :], preferred_element_type=F32).astype(BF16)
        for c in range(ways):
            out_ref[k * block : (k + 1) * block, c * 128 : (c + 1) * 128] = laid[c * block : (c + 1) * block, :]


def lay_qkv(w_qkv):
    depth, heads, three, dim = w_qkv.shape
    ways = heads * three
    turned = w_qkv.transpose(0, 2, 1, 3)
    if heads != 2 or dim != 128 or depth % 512:
        return turned.reshape(depth, ways * dim)
    return pl.pallas_call(
        functools.partial(lay_kernel, ways),
        out_shape=jax.ShapeDtypeStruct((depth, ways * dim), BF16),
        grid=(depth // 512,),
        in_specs=[pl.BlockSpec((512 * ways, dim), lambda i: (i, 0))],
        out_specs=pl.BlockSpec((512, ways * dim), lambda i: (i, 0)),
        cost_estimate=pl.CostEstimate(flops=2 * depth * ways * dim * 384, bytes_accessed=4 * depth * ways * dim, transcendentals=0),
    )(turned.reshape(depth * ways, dim))


def head_norm(values_in, gain):
    width_count = values_in.shape[-1]
    row_mean = jnp.sum(values_in, -1, keepdims=True) / width_count
    row_var = jnp.sum(values_in * values_in, -1, keepdims=True) / width_count - row_mean * row_mean
    return (values_in - row_mean) * lax.rsqrt(row_var + 1e-06) * gain


def attention(qkv, q_gain, k_gain):
    heads, dim = q_gain.shape
    count = qkv.shape[0] // PATCHES
    parts = qkv.reshape(count, PATCHES, 3, heads, dim)
    queries = head_norm(parts[:, :, 0], q_gain).astype(BF16)
    keys_normed = head_norm(parts[:, :, 1], k_gain).astype(BF16)
    values = parts[:, :, 2].astype(BF16)
    scores = jnp.einsum("iphd,iqhd->ihpq", queries, keys_normed, preferred_element_type=F32) / jnp.sqrt(F32(dim))
    expo = jnp.exp(scores - jnp.max(scores, -1, keepdims=True))
    weights = (expo / jnp.sum(expo, -1, keepdims=True)).astype(BF16)
    attended = jnp.einsum("ihpq,iqhd->iphd", weights, values, preferred_element_type=F32)
    return attended.astype(BF16).reshape(-1, heads * dim)


def any_mesh(
    tokens, ln_gain, oft_skew, tenant_of_image, w_qkv, w_up, up_bias, q_gain, k_gain, w_out, w_down, down_bias
):
    row_count, local_width = tokens.shape
    ways = lax.axis_size("gy")
    full_width = local_width * ways
    gx, gy = lax.axis_index("gx"), lax.axis_index("gy")
    dot = functools.partial(jnp.dot, preferred_element_type=F32)

    tenant = lax.dynamic_index_in_dim(tenant_of_image, gx * row_count // PATCHES, 0, keepdims=False)
    rotation = turning(oft_skew, tenant)
    floats = tokens.astype(F32)
    sums = jnp.stack([jnp.sum(floats, 1), jnp.sum(floats * floats, 1)])
    sums = lax.psum(sums, "gy")
    row_mean = sums[0][:, None] / full_width
    row_var = sums[1][:, None] / full_width - row_mean * row_mean
    normed = (floats - row_mean) * lax.rsqrt(row_var + 1e-06) * ln_gain
    count, size = rotation.shape[:2]
    turned = jnp.einsum("pnb,nbc->pnc", normed.reshape(row_count, count, size), rotation, precision=HIGH)
    turned = turned.reshape(row_count, local_width).astype(BF16)
    w_first = lay_qkv(w_qkv)
    every = lax.all_gather(turned, "gx", axis=0, tiled=True)

    qkv_cols, up_cols = w_first.shape[1], w_up.shape[1]
    w_attn = w_out.reshape(-1, w_out.shape[2])
    part = jnp.concatenate([dot(every, w_first), dot(every, w_up)], 1)
    summed = lax.psum_scatter(part.astype(BF16), "gy", scatter_dimension=0, tiled=True).astype(F32)
    acts = jnp.concatenate(
        [
            attention(summed[:, :qkv_cols], q_gain, k_gain),
            jax.nn.gelu(summed[:, qkv_cols:] + up_bias, approximate=False).astype(BF16),
        ],
        1,
    )
    acts = lax.all_gather(acts, "gy", axis=0, tiled=True)
    heads_cols = w_attn.shape[0]
    mixed = (dot(acts[:, :heads_cols], w_attn) + dot(acts[:, heads_cols:], w_down)).astype(BF16)
    mixed = lax.psum_scatter(mixed, "gx", scatter_dimension=0, tiled=True)
    return (floats + mixed.astype(F32) + down_bias).astype(BF16)


def swap_gy(a):
    return lax.ppermute(a, "gy", [(0, 1), (1, 0)])


def swap_gx(a, bit):
    return lax.ppermute(a, "gx", [(i, i ^ bit) for i in range(16)])


def pair(bit_set, mine, got, axis):
    return jnp.concatenate([jnp.where(bit_set, got, mine), jnp.where(bit_set, mine, got)], axis)


def small_mesh(
    tokens, ln_gain, oft_skew, tenant_of_image, w_qkv, w_up, up_bias, q_gain, k_gain, w_out, w_down, down_bias
):
    rows, width = tokens.shape
    gx, gy = lax.axis_index("gx"), lax.axis_index("gy")
    core, y_bit, z_high = gx % 2, (gx // 2) % 2, gx // 8
    dot = functools.partial(jnp.dot, preferred_element_type=F32)
    half, quarter = width // 2, width // 4

    tenant = lax.dynamic_index_in_dim(tenant_of_image, gx * rows // PATCHES, 0, keepdims=False)
    rotation = turning(oft_skew, tenant, 4, core * 2 + y_bit)
    floats = tokens.astype(F32)
    sums = jnp.stack([jnp.sum(floats, 1), jnp.sum(floats * floats, 1)])
    sums = sums + swap_gy(sums)
    row_mean = sums[0][:, None] / (2 * width)
    row_var = sums[1][:, None] / (2 * width) - row_mean * row_mean
    normed = (floats - row_mean) * lax.rsqrt(row_var + 1e-06) * ln_gain

    def part(a, index, size):
        return lax.dynamic_slice_in_dim(a, index * size, size, 1)

    block = pair(core == 1, part(normed, core, half), swap_gx(part(normed, 1 - core, half), 1), 0)
    block = pair(y_bit == 1, part(block, y_bit, quarter), swap_gx(part(block, 1 - y_bit, quarter), 2), 0)
    count, size = rotation.shape[:2]
    turned = jnp.einsum("pnb,nbc->pnc", block.reshape(4 * rows, count, size), rotation, precision=HIGH)
    turned = turned.reshape(4 * rows, quarter).astype(BF16)
    w_first = lay_qkv(w_qkv)

    cut = quarter // 2
    strips = []
    for s in range(2):
        a = turned[None, None, :, s * cut : (s + 1) * cut]
        a = jnp.concatenate([a, swap_gx(a, 8)], 0)
        a = jnp.concatenate([a, swap_gx(a, 4)], 1)
        a = a.reshape(2, 8 * rows, 1, cut)
        got = swap_gx(a, 2)
        a = pair(y_bit == 1, a, got, 2)
        got = swap_gx(a, 1)
        strips.append(pair(core == 1, a, got, 2))
    every = jnp.stack(strips, 3).reshape(2, 8 * rows, width)
    mine = lax.dynamic_index_in_dim(every, z_high ^ gy, 0, keepdims=False)
    theirs = lax.dynamic_index_in_dim(every, z_high ^ gy ^ 1, 0, keepdims=False)

    w_attn = w_out.reshape(-1, w_out.shape[2])
    third = w_up.shape[1] // 3
    pieces = [w_first] + [w_up[:, k * third : (k + 1) * third] for k in range(3)]
    got = [swap_gy(dot(theirs, w).astype(BF16)) for w in pieces]
    own = [dot(mine, w) for w in pieces]
    summed = [a + b.astype(F32) for a, b in zip(own, got)]
    acts = [attention(summed[0], q_gain, k_gain)]
    for k in range(3):
        pre = summed[k + 1] + up_bias[k * third : (k + 1) * third]
        acts.append(jax.nn.gelu(pre, approximate=False).astype(BF16))
    others = [swap_gy(a) for a in acts]

    def reduced(attended, hidden, cols):
        a = dot(attended, w_attn[:, cols]) + dot(hidden, w_down[:, cols])
        a = a.reshape(2, 2, 2, rows, -1)
        sent = lax.dynamic_index_in_dim(a, 1 - core, 2, keepdims=False).astype(BF16)
        a = lax.dynamic_index_in_dim(a, core, 2, keepdims=False) + swap_gx(sent, 1).astype(F32)
        sent = lax.dynamic_index_in_dim(a, 1 - y_bit, 1, keepdims=False).astype(BF16)
        a = lax.dynamic_index_in_dim(a, y_bit, 1, keepdims=False) + swap_gx(sent, 2).astype(F32)
        return a[0] + swap_gx(a[1].astype(BF16), 4).astype(F32)

    spans = [slice(0, half), slice(half, width)]
    hidden = jnp.concatenate(acts[1:], 1)
    first = [reduced(acts[0], hidden, cols) for cols in spans]
    hidden = jnp.concatenate(others[1:], 1)
    second = [reduced(others[0], hidden, cols) for cols in spans]
    here = z_high == gy
    mixed = []
    for a, b in zip(first, second):
        mixed.append(jnp.where(here, a, b) + swap_gx(jnp.where(here, b, a).astype(BF16), 8).astype(F32))
    return (floats + jnp.concatenate(mixed, 1) + down_bias).astype(BF16)


def solution(mesh):
    in_specs = (
        P("gx", "gy"),
        P("gy"),
        P(None, "gy", None, None),
        P(),
        P("gy", "gx", None, None),
        P("gy", "gx"),
        P("gx"),
        P("gx", None),
        P("gx", None),
        P("gx", None, "gy"),
        P("gx", "gy"),
        P("gy"),
    )
    small = dict(mesh.shape) == {"gx": 16, "gy": 2}
    per_device = small_mesh if small else any_mesh
    return jax.shard_map(per_device, mesh=mesh, in_specs=in_specs, out_specs=P("gx", "gy"), check_vma=False)
```

```python
import functools

import jax
import jax.numpy as jnp
from jax import lax
from jax.experimental import pallas as pl
from jax.experimental.pallas import tpu as pltpu
from jax.sharding import PartitionSpec as P

PATCHES = 256
HIGH = lax.Precision.HIGHEST
F32 = jnp.float32
BF16 = jnp.bfloat16


def split(a):
    high = a.astype(BF16)
    return high, (a - high.astype(F32)).astype(BF16)


def dot3(a, b):
    dot = functools.partial(jnp.dot, preferred_element_type=F32)
    return dot(a[0], b[0]) + (dot(a[0], b[1]) + dot(a[1], b[0]))


def inverse_kernel(per, tenant_ref, skew_ref, out_ref, gen_hi, gen_lo, x_ref):
    size = skew_ref.shape[-1]
    rows = lax.broadcasted_iota(jnp.int32, (size, size), 0)
    cols = lax.broadcasted_iota(jnp.int32, (size, size), 1)
    eye = (rows == cols).astype(F32)
    bound = jnp.float32(0.0)
    for k in range(per):
        raw = skew_ref[0, k]
        skew = 0.5 * (raw - raw.T)
        pair = split(skew)
        square = dot3(pair, pair)
        bound = jnp.maximum(bound, jnp.sum(square * square))
        whole = split(eye + skew)
        gen_hi[k] = whole[0]
        gen_lo[k] = whole[1]
        x_ref[k] = eye - skew
    top = 1.001 * jnp.sqrt(jnp.full((8, 128), 0.5 * bound, F32)) + 1e-3
    low = 2.0 / (2.0 + top)
    for k in range(per):
        x_ref[k] = x_ref[k] * low[0:1, 0:1]

    def more(state):
        return state[1] < 1.0 - 1e-6

    def step(state):
        low, _ = state
        grown = low * (2.0 - low)
        scale = 2.0 / (1.0 + grown)
        xs = [split(x_ref[k]) for k in range(per)]
        ys = [dot3((gen_hi[k], gen_lo[k]), xs[k]) for k in range(per)]
        rest = [split(2.0 * eye - y) for y in ys]
        for k in range(per):
            x_ref[k] = dot3(xs[k], rest[k]) * scale[0:1, 0:1]
        low = jnp.minimum(scale * grown, 1.0)
        return low, jnp.max(low)

    lax.while_loop(more, step, (low, jnp.max(low)))
    for k in range(per):
        out_ref[k] = 2.0 * x_ref[k] - eye


def turning(oft_skew, tenant, shares=1, share=0):
    _, count, size, _ = oft_skew.shape
    count = count // shares
    per = next(p for p in (4, 3, 2, 1) if count % p == 0)
    return pl.pallas_call(
        functools.partial(inverse_kernel, per),
        out_shape=jax.ShapeDtypeStruct((count, size, size), F32),
        grid_spec=pltpu.PrefetchScalarGridSpec(
            num_scalar_prefetch=1,
            grid=(count // per,),
            in_specs=[pl.BlockSpec((1, per, size, size), lambda i, t: (t[0], t[1] + i, 0, 0))],
            out_specs=pl.BlockSpec((per, size, size), lambda i, t: (i, 0, 0)),
            scratch_shapes=[
                pltpu.VMEM((per, size, size), BF16),
                pltpu.VMEM((per, size, size), BF16),
                pltpu.VMEM((per, size, size), F32),
            ],
        ),
        compiler_params=pltpu.CompilerParams(vmem_limit_bytes=32 * 2**20),
        cost_estimate=pl.CostEstimate(flops=count * 50 * 2 * size**3, bytes_accessed=count * 8 * size**2, transcendentals=0),
    )(jnp.stack([tenant, jnp.int32(share * (count // per))]), oft_skew)


def lay_kernel(ways, w_ref, out_ref):
    block = 64
    size = ways * block
    rows = lax.broadcasted_iota(jnp.int32, (size, size), 0)
    cols = lax.broadcasted_iota(jnp.int32, (size, size), 1)
    move = (cols == (rows % block) * ways + rows // block).astype(BF16)
    for k in range(out_ref.shape[0] // block):
        laid = jnp.dot(move, w_ref[k * size : (k + 1) * size, :], preferred_element_type=F32).astype(BF16)
        for c in range(ways):
            out_ref[k * block : (k + 1) * block, c * 128 : (c + 1) * 128] = laid[c * block : (c + 1) * block, :]


def lay_qkv(w_qkv):
    depth, heads, three, dim = w_qkv.shape
    ways = heads * three
    turned = w_qkv.transpose(0, 2, 1, 3)
    if heads != 2 or dim != 128 or depth % 512:
        return turned.reshape(depth, ways * dim)
    return pl.pallas_call(
        functools.partial(lay_kernel, ways),
        out_shape=jax.ShapeDtypeStruct((depth, ways * dim), BF16),
        grid=(depth // 512,),
        in_specs=[pl.BlockSpec((512 * ways, dim), lambda i: (i, 0))],
        out_specs=pl.BlockSpec((512, ways * dim), lambda i: (i, 0)),
        cost_estimate=pl.CostEstimate(flops=2 * depth * ways * dim * 384, bytes_accessed=4 * depth * ways * dim, transcendentals=0),
    )(turned.reshape(depth * ways, dim))


def head_norm(values_in, gain):
    width_count = values_in.shape[-1]
    row_mean = jnp.sum(values_in, -1, keepdims=True) / width_count
    row_var = jnp.sum(values_in * values_in, -1, keepdims=True) / width_count - row_mean * row_mean
    return (values_in - row_mean) * lax.rsqrt(row_var + 1e-06) * gain


def attention(qkv, q_gain, k_gain):
    heads, dim = q_gain.shape
    count = qkv.shape[0] // PATCHES
    parts = qkv.reshape(count, PATCHES, 3, heads, dim)
    queries = head_norm(parts[:, :, 0], q_gain).astype(BF16)
    keys_normed = head_norm(parts[:, :, 1], k_gain).astype(BF16)
    values = parts[:, :, 2].astype(BF16)
    scores = jnp.einsum("iphd,iqhd->ihpq", queries, keys_normed, preferred_element_type=F32) / jnp.sqrt(F32(dim))
    expo = jnp.exp(scores - jnp.max(scores, -1, keepdims=True))
    weights = (expo / jnp.sum(expo, -1, keepdims=True)).astype(BF16)
    attended = jnp.einsum("ihpq,iqhd->iphd", weights, values, preferred_element_type=F32)
    return attended.astype(BF16).reshape(-1, heads * dim)


def any_mesh(
    tokens, ln_gain, oft_skew, tenant_of_image, w_qkv, w_up, up_bias, q_gain, k_gain, w_out, w_down, down_bias
):
    row_count, local_width = tokens.shape
    ways = lax.axis_size("gy")
    full_width = local_width * ways
    gx, gy = lax.axis_index("gx"), lax.axis_index("gy")
    dot = functools.partial(jnp.dot, preferred_element_type=F32)

    tenant = lax.dynamic_index_in_dim(tenant_of_image, gx * row_count // PATCHES, 0, keepdims=False)
    rotation = turning(oft_skew, tenant)
    floats = tokens.astype(F32)
    sums = jnp.stack([jnp.sum(floats, 1), jnp.sum(floats * floats, 1)])
    sums = lax.psum(sums, "gy")
    row_mean = sums[0][:, None] / full_width
    row_var = sums[1][:, None] / full_width - row_mean * row_mean
    normed = (floats - row_mean) * lax.rsqrt(row_var + 1e-06) * ln_gain
    count, size = rotation.shape[:2]
    turned = jnp.einsum("pnb,nbc->pnc", normed.reshape(row_count, count, size), rotation, precision=HIGH)
    turned = turned.reshape(row_count, local_width).astype(BF16)
    w_first = lay_qkv(w_qkv)
    every = lax.all_gather(turned, "gx", axis=0, tiled=True)

    qkv_cols, up_cols = w_first.shape[1], w_up.shape[1]
    w_attn = w_out.reshape(-1, w_out.shape[2])
    part = jnp.concatenate([dot(every, w_first), dot(every, w_up)], 1)
    summed = lax.psum_scatter(part.astype(BF16), "gy", scatter_dimension=0, tiled=True).astype(F32)
    acts = jnp.concatenate(
        [
            attention(summed[:, :qkv_cols], q_gain, k_gain),
            jax.nn.gelu(summed[:, qkv_cols:] + up_bias, approximate=False).astype(BF16),
        ],
        1,
    )
    acts = lax.all_gather(acts, "gy", axis=0, tiled=True)
    heads_cols = w_attn.shape[0]
    mixed = (dot(acts[:, :heads_cols], w_attn) + dot(acts[:, heads_cols:], w_down)).astype(BF16)
    mixed = lax.psum_scatter(mixed, "gx", scatter_dimension=0, tiled=True)
    return (floats + mixed.astype(F32) + down_bias).astype(BF16)


def swap_gy(a):
    return lax.ppermute(a, "gy", [(0, 1), (1, 0)])


def swap_gx(a, bit):
    return lax.ppermute(a, "gx", [(i, i ^ bit) for i in range(16)])


def pair(bit_set, mine, got, axis):
    return jnp.concatenate([jnp.where(bit_set, got, mine), jnp.where(bit_set, mine, got)], axis)


def small_mesh(
    tokens, ln_gain, oft_skew, tenant_of_image, w_qkv, w_up, up_bias, q_gain, k_gain, w_out, w_down, down_bias
):
    rows, width = tokens.shape
    gx, gy = lax.axis_index("gx"), lax.axis_index("gy")
    core, y_bit, z_high = gx % 2, (gx // 2) % 2, gx // 8
    dot = functools.partial(jnp.dot, preferred_element_type=F32)
    half, quarter = width // 2, width // 4

    tenant = lax.dynamic_index_in_dim(tenant_of_image, gx * rows // PATCHES, 0, keepdims=False)
    rotation = turning(oft_skew, tenant, 4, core * 2 + y_bit)
    floats = tokens.astype(F32)
    sums = jnp.stack([jnp.sum(floats, 1), jnp.sum(floats * floats, 1)])
    sums = sums + swap_gy(sums)
    row_mean = sums[0][:, None] / (2 * width)
    row_var = sums[1][:, None] / (2 * width) - row_mean * row_mean
    normed = (floats - row_mean) * lax.rsqrt(row_var + 1e-06) * ln_gain

    def part(a, index, size):
        return lax.dynamic_slice_in_dim(a, index * size, size, 1)

    block = pair(core == 1, part(normed, core, half), swap_gx(part(normed, 1 - core, half), 1), 0)
    block = pair(y_bit == 1, part(block, y_bit, quarter), swap_gx(part(block, 1 - y_bit, quarter), 2), 0)
    count, size = rotation.shape[:2]
    turned = jnp.einsum("pnb,nbc->pnc", block.reshape(4 * rows, count, size), rotation, precision=HIGH)
    turned = turned.reshape(4 * rows, quarter).astype(BF16)
    w_first = lay_qkv(w_qkv)

    cut = quarter // 2
    strips = []
    for s in range(2):
        a = turned[None, None, :, s * cut : (s + 1) * cut]
        a = jnp.concatenate([a, swap_gx(a, 8)], 0)
        a = jnp.concatenate([a, swap_gx(a, 4)], 1)
        a = a.reshape(2, 8 * rows, 1, cut)
        got = swap_gx(a, 2)
        if s == 0:
            got, w_first = lax.optimization_barrier((got, w_first))
        a = pair(y_bit == 1, a, got, 2)
        got = swap_gx(a, 1)
        strips.append(pair(core == 1, a, got, 2))
    every = jnp.stack(strips, 3).reshape(2, 8 * rows, width)
    mine = lax.dynamic_index_in_dim(every, z_high ^ gy, 0, keepdims=False)
    theirs = lax.dynamic_index_in_dim(every, z_high ^ gy ^ 1, 0, keepdims=False)

    w_attn = w_out.reshape(-1, w_out.shape[2])
    third = w_up.shape[1] // 3
    pieces = [w_first] + [w_up[:, k * third : (k + 1) * third] for k in range(3)]
    got = [swap_gy(dot(theirs, w).astype(BF16)) for w in pieces]
    own = [lax.optimization_barrier(dot(mine, w)) for w in pieces]
    acts = [attention(own[0] + got[0].astype(F32), q_gain, k_gain)]
    got[2], acts[0] = lax.optimization_barrier((got[2], acts[0]))
    for k in range(3):
        pre = own[k + 1] + got[k + 1].astype(F32) + up_bias[k * third : (k + 1) * third]
        acts.append(jax.nn.gelu(pre, approximate=False).astype(BF16))
    others = [swap_gy(a) for a in acts]

    def reduced(attended, hidden, cols):
        a = dot(attended, w_attn[:, cols]) + dot(hidden, w_down[:, cols])
        a = a.reshape(2, 2, 2, rows, -1)
        sent = lax.dynamic_index_in_dim(a, 1 - core, 2, keepdims=False).astype(BF16)
        a = lax.dynamic_index_in_dim(a, core, 2, keepdims=False) + swap_gx(sent, 1).astype(F32)
        sent = lax.dynamic_index_in_dim(a, 1 - y_bit, 1, keepdims=False).astype(BF16)
        a = lax.dynamic_index_in_dim(a, y_bit, 1, keepdims=False) + swap_gx(sent, 2).astype(F32)
        return a[0] + swap_gx(a[1].astype(BF16), 4).astype(F32)

    spans = [slice(0, half), slice(half, width)]
    hidden = jnp.concatenate(acts[1:], 1)
    first = [reduced(acts[0], hidden, cols) for cols in spans]
    hidden = jnp.concatenate(others[1:], 1)
    second = [reduced(others[0], hidden, cols) for cols in spans]
    here = z_high == gy
    mixed = []
    for a, b in zip(first, second):
        mixed.append(jnp.where(here, a, b) + swap_gx(jnp.where(here, b, a).astype(BF16), 8).astype(F32))
    return (floats + jnp.concatenate(mixed, 1) + down_bias).astype(BF16)


def solution(mesh):
    in_specs = (
        P("gx", "gy"),
        P("gy"),
        P(None, "gy", None, None),
        P(),
        P("gy", "gx", None, None),
        P("gy", "gx"),
        P("gx"),
        P("gx", None),
        P("gx", None),
        P("gx", None, "gy"),
        P("gx", "gy"),
        P("gy"),
    )
    small = dict(mesh.shape) == {"gx": 16, "gy": 2}
    per_device = small_mesh if small else any_mesh
    return jax.shard_map(per_device, mesh=mesh, in_specs=in_specs, out_specs=P("gx", "gy"), check_vma=False)
```
